32 devices in a mesh: replica: 2 (over y), hidden: 2 (over x), expert: 4 (over z), request: 2 (over core).
Axes of the slice: x: 2, y: 2, z: 4, core: 2. Of those that a mesh axis runs over, the one named last changes fastest.
Arguments:
- tokens: bfloat16 [256, 3072], P(('replica', 'expert', 'request'), 'hidden'), parts along dimension 0, may hold values from -6 to 6
- expert_ids: int32 [256, 2], P(('replica', 'expert', 'request')), parts along dimension 0, may hold values from 0 to 3, all different within a row; in each aligned block of 16 rows (0 to 15, 16 to 31, ...) at most 16 rows name the same one
- gate_weights: float32 [256, 2], P(('replica', 'expert', 'request')), parts along dimension 0, may hold values from 0.2 to 1
- w_gate: bfloat16 [4, 3072, 8192], P('expert', None, ('hidden', 'request')), may hold values from -0.109375 to 0.109375
- w_up: bfloat16 [4, 3072, 8192], P('expert', None, ('hidden', 'request')), may hold values from -0.109375 to 0.109375
- w_down: bfloat16 [4, 8192, 3072], P('expert', ('hidden', 'request')), may hold values from -0.09375 to 0.09375
Outputs:
- combined: bfloat16 [256, 3072], P(('replica', 'expert', 'request'), 'hidden'), parts along dimension 0
The draws below stay inside these ranges and needn't reach their ends.
There are 2 independent parts, one for each index of `replica`. The reference program is written for one: setup_inputs(seed, part) draws one part's arguments, and reference() takes and returns one part's arrays. A program takes and returns all parts, laid end to end along the dimension named above; an argument that names none is the same for every part. Nothing has to cross between parts.
Inputs may be any that keep to these rules, and one draw needn't show every extreme that they name: `expert_ids`: the two experts of a row differ. In each aligned block of 16 rows (the rows of one device) no expert is named by more than 16 rows, a bound that some block reaches.
All inputs are finite; a program needn't handle non-finite values.
Results may differ from the reference program's by a relative error of at most 0.0057.
Values may be sent and summed in bfloat16 or wider, within the bound.
No kernel may reach another device: no remote copies, remote signals or barrier semaphores. Data moves between devices by JAX's collectives and lax.ppermute only.
A program may use at most 128 MiB of HBM per device.

```python
import math
import jax
import jax.numpy as jnp
import numpy as np

D = 3072
FF = 8192
TOK_DEV = 16
EXPERTS = 4
CAP = 16
TOKENS = 128
N_EXPERT = 4
N_REQUEST = 2


def spiked(entries, stream_key, source, target, parts, factor):
    owner, partner = [(jnp.arange(entries.shape[position]) // (entries.shape[position] // parts)).reshape([-1 if axis == position else 1 for axis in range(entries.ndim)]) for position in (source, target)]
    chosen = jax.random.permutation(stream_key, parts)[partner]
    strong = (owner == chosen) | (owner == (partner + parts // 2) % parts)
    return jnp.where(strong, factor * entries, entries)


def steps_of(own_key, extent, shards, least, largest):
    def one(dim, blocks):
        heights = jax.random.uniform(jax.random.fold_in(jax.random.fold_in(own_key, 6), dim), (blocks,), jnp.float32, least / len(shards), largest / len(shards))
        return jnp.repeat(jnp.exp(heights), extent[dim] // blocks).reshape((-1,) + (1,) * (len(extent) - dim - 1))

    level = one(*shards[0])
    for cut in shards[1:]:
        level = level * one(*cut)
    return level


def shared_out(key, own, number, rows, number_of, top, most, slope):
    sequence = jax.random.permutation(key, number_of)
    crowded, ordinary = portions_of(number_of, rows * top, most, slope, True), portions_of(number_of, rows * top, most, slope, False)
    places = jnp.arange(number_of)

    def named(tallies, offset_by):
        used = int((tallies > 0).sum())
        fixed = max(1, used // 4)
        passed = fixed + (places - fixed + offset_by * (used - fixed)) % max(1, number_of - fixed)
        return jnp.zeros((number_of,), jnp.int32).at[sequence[jnp.where(places < fixed, places, passed)]].set(jnp.asarray(tallies, jnp.int32))

    tallies = jnp.where(number % 4 == 0, named(crowded, number // 4), named(ordinary, number - number // 4 - 1))
    mixed = jax.random.permutation(jax.random.fold_in(own, 3), number_of)
    donor, receiver = mixed[0:number_of // 2 * 2:2], mixed[1:number_of // 2 * 2:2]
    slack = jnp.minimum(tallies[donor] - 1, most - tallies[receiver]) // 2
    slack = jnp.where((donor == sequence[0]) | (receiver == sequence[0]) | (tallies[receiver] == 0), 0, jnp.maximum(slack, 0))
    passed = jax.random.randint(jax.random.fold_in(own, 4), (number_of // 2,), 0, 1 << 20) % (slack + 1)
    tallies = tallies.at[donor].add(-passed).at[receiver].add(passed)
    items = jnp.searchsorted(jnp.cumsum(tallies), jnp.arange(rows * top), side="right").astype(jnp.int32)
    listing = items.reshape(top, rows).T
    listing = listing[jax.random.permutation(jax.random.fold_in(own, 1), rows)]
    offset_by = jax.random.randint(jax.random.fold_in(own, 2), (rows, 1), 0, top)
    return jnp.take_along_axis(listing, (jnp.arange(top)[None, :] + offset_by) % top, axis=1)


def portions_of(amount, total, limit, lean, full):
    portions = [(1 << 20) // math.isqrt(standing ** lean) + 1 for standing in range(1, amount + 1)]
    largest = limit if full else min(limit, max(-(-total // amount), total * portions[0] // sum(portions)))
    least = 1 if total - largest >= amount - 1 else 0
    counts, spare = [largest] + [least] * (amount - 1), total - largest - least * (amount - 1)
    while spare > 0:
        movable = [i for i in range(1, amount) if counts[i] < largest] or [i for i in range(1, amount) if counts[i] < limit]
        mass, remaining = sum([portions[i] for i in movable]), spare
        for i in movable:
            extra = min(limit - counts[i], max(1, remaining * portions[i] // mass), spare)
            counts[i] = counts[i] + extra
            spare = spare - extra
    return np.array(counts)


def gaussian(stream_key, shape, scale, reach, pieces=(), kind=jnp.bfloat16):
    entries = scale * jax.random.normal(stream_key, shape, jnp.float32)
    if pieces:
        entries = entries * steps_of(stream_key, shape, pieces, -0.22, 0.18)
    return jnp.clip(entries, -reach, reach).astype(kind)


def noise_with(own_key, shape, deviation, reach, cuts, heavy, held_as=jnp.bfloat16):
    drawn = deviation * jax.random.normal(own_key, shape, jnp.float32)
    if cuts:
        drawn = drawn * steps_of(own_key, shape, cuts, -0.22, 0.18)
    return jnp.clip(spiked(drawn, jax.random.fold_in(own_key, 3), *heavy), -reach, reach).astype(held_as)


def setup_inputs(seed: int = 0, part: int = 0) -> dict:
    splits = jax.random.split(jax.random.key(seed), 7)
    own_keys = jax.random.split(jax.random.fold_in(splits[6], part), 7)
    tokens = gaussian(own_keys[0], (TOKENS, D), 1.0, 6.0, ((0, 8), (1, 2)))
    expert_ids_keys = jax.random.split(jax.random.fold_in(own_keys[1], 1), TOKENS // TOK_DEV)
    expert_ids_turns = jax.random.permutation(jax.random.fold_in(own_keys[1], 3), TOKENS // TOK_DEV)
    expert_ids = jax.vmap(lambda own, number: shared_out(jax.random.fold_in(own_keys[1], 2), own, number, TOK_DEV, EXPERTS, 2, CAP, 2))(expert_ids_keys, expert_ids_turns).reshape((TOKENS, 2))
    gate_weights = jnp.clip(0.2 + 0.8 * jax.random.uniform(own_keys[2], (TOKENS, 2), jnp.float32) ** steps_of(own_keys[2], (TOKENS, 2), ((0, 8),), -0.2, 0.2), 0.2, 1.0)
    w_gate = gaussian(splits[3], (EXPERTS, D, FF), D ** -0.5, 0.109375, ((0, 4), (2, 4)))
    w_up = gaussian(splits[4], (EXPERTS, D, FF), D ** -0.5, 0.109375, ((0, 4), (2, 4)))
    w_down = noise_with(splits[5], (EXPERTS, FF, D), FF ** -0.5, 0.09375, ((0, 4), (1, 4)), (1, 2, 4, 2.0))
    return {"tokens": tokens, "expert_ids": expert_ids, "gate_weights": gate_weights, "w_gate": w_gate, "w_up": w_up, "w_down": w_down}


def reference(tokens, expert_ids, gate_weights, w_gate, w_up, w_down):
    max_rows = N_EXPERT * N_REQUEST * CAP
    combined = jnp.zeros((tokens.shape[0], tokens.shape[1]), jnp.float32)
    for expert in range(EXPERTS):
        chosen = expert_ids == expert
        weight_row = jnp.sum(jnp.where(chosen, gate_weights, jnp.zeros_like(gate_weights)), axis=1)
        picked = jnp.any(chosen, axis=1)
        positions = jnp.nonzero(picked, size=max_rows, fill_value=0)[0].astype(jnp.int32)
        live_slots = jnp.arange(max_rows, dtype=jnp.int32) < jnp.sum(picked.astype(jnp.int32))
        selected = tokens[positions]
        gate_part = jnp.dot(selected, w_gate[expert], preferred_element_type=jnp.float32)
        up_part = jnp.dot(selected, w_up[expert], preferred_element_type=jnp.float32)
        activation = (jax.nn.silu(gate_part) * up_part).astype(jnp.bfloat16)
        expert_out = jnp.dot(activation, w_down[expert], preferred_element_type=jnp.float32).astype(jnp.bfloat16)
        slot_scale = jnp.where(live_slots, weight_row[positions], jnp.zeros_like(weight_row[positions]))
        combined = combined.at[positions].add(slot_scale[:, None] * expert_out.astype(combined.dtype))
    return combined.astype(jnp.bfloat16)
```

```python
import functools

import jax
import jax.numpy as jnp
from jax import lax
from jax.experimental import pallas as pl
from jax.experimental.pallas import tpu as pltpu
from jax.sharding import PartitionSpec as P

F32 = jnp.float32
BF16 = jnp.bfloat16
VMEM_SPEC = pl.BlockSpec(memory_space=pltpu.VMEM)
HBM_SPEC = pl.BlockSpec(memory_space=pltpu.HBM)


def shift(x, axis, by):
    size = lax.axis_size(axis)
    return lax.ppermute(x, axis, [(i, (i + by) % size) for i in range(size)])


def in_hbm(x):
    return pltpu.with_memory_space_constraint(x, pltpu.HBM)


def in_vmem(x):
    return pltpu.with_memory_space_constraint(x, pltpu.VMEM)


def load_kernel(half, w_ref, after_ref, out_ref, sems):
    mine = lax.axis_index("hidden")
    copies = []
    for part in range(2):
        start = pl.multiple_of((mine if part == 0 else 1 - mine) * half, half)
        copies.append(
            pltpu.make_async_copy(
                w_ref.at[pl.ds(start, half)], out_ref.at[pl.ds(part * half, half)], sems.at[part]
            )
        )
    for copy in copies:
        copy.start()
    for copy in copies:
        copy.wait()


def load(w, after):
    rows, cols = w.shape
    return pl.pallas_call(
        functools.partial(load_kernel, rows // 2),
        out_shape=pltpu.VMEM(w.shape, w.dtype),
        in_specs=[HBM_SPEC, pl.BlockSpec(memory_space=pl.ANY)],
        out_specs=VMEM_SPEC,
        scratch_shapes=[pltpu.SemaphoreType.DMA((2,))],
        compiler_params=pltpu.CompilerParams(vmem_limit_bytes=2**20),
        name="load",
    )(in_hbm(w), after)


def hidden_kernel(
    block, x00, x01, x10, x11, gate_ref, up_ref, down_hbm,
    act_ref, down_mine, keep_ref, send_ref, x_ref, down_other, sems,
):
    mine = lax.axis_index("hidden")
    rows, half = x00.shape
    copies = []
    for part, dst in ((1, down_other), (0, down_mine)):
        start = pl.multiple_of((mine if part == 0 else 1 - mine) * half, 128)
        copies.append(
            pltpu.make_async_copy(down_hbm.at[:, pl.ds(start, half)], dst, sems.at[part])
        )
    for copy in copies:
        copy.start()
    x_ref[0:rows, 0:half] = x00[...]
    x_ref[0:rows, half:] = x01[...]
    x_ref[rows:, 0:half] = x10[...]
    x_ref[rows:, half:] = x11[...]
    x = x_ref[...]
    for j in range(gate_ref.shape[1] // block):
        s = slice(j * block, (j + 1) * block)
        gate = jnp.dot(x, gate_ref[:, s], preferred_element_type=F32)
        up = jnp.dot(x, up_ref[:, s], preferred_element_type=F32)
        act_ref[:, s] = (gate / (1.0 + jnp.exp(-gate)) * up).astype(BF16)
    copies[0].wait()
    act = act_ref[...]
    for j in range(half // block):
        s = slice(j * block, (j + 1) * block)
        out = jnp.dot(act, down_other[:, s], preferred_element_type=F32)
        keep_ref[:, s] = out[:rows]
        send_ref[:, s] = out[rows:].astype(BF16)
    copies[1].wait()


def hidden_part(x00, x01, x10, x11, gate, up, down):
    rows, half = x00.shape
    ff = gate.shape[1]
    return pl.pallas_call(
        functools.partial(hidden_kernel, 512),
        out_shape=[
            pltpu.VMEM((2 * rows, ff), BF16),
            pltpu.VMEM((ff, half), BF16),
            pltpu.VMEM((rows, half), F32),
            pltpu.VMEM((rows, half), BF16),
        ],
        in_specs=[VMEM_SPEC] * 6 + [HBM_SPEC],
        out_specs=[VMEM_SPEC] * 4,
        scratch_shapes=[
            pltpu.VMEM((2 * rows, 2 * half), BF16),
            pltpu.VMEM((ff, half), BF16),
            pltpu.SemaphoreType.DMA((2,)),
        ],
        compiler_params=pltpu.CompilerParams(vmem_limit_bytes=14 * 2**20),
        name="hidden",
    )(x00, x01, x10, x11, in_vmem(gate), in_vmem(up), in_hbm(down))


def down_kernel(block, act_ref, down_ref, keep_ref, send_ref):
    rows, half = keep_ref.shape
    act = act_ref[...]
    for j in range(half // block):
        s = slice(j * block, (j + 1) * block)
        out = jnp.dot(act, down_ref[:, s], preferred_element_type=F32)
        keep_ref[:, s] = out[:rows]
        send_ref[:, s] = out[rows:].astype(BF16)


def down_part(act, down):
    rows, half = act.shape[0] // 2, down.shape[1]
    return pl.pallas_call(
        functools.partial(down_kernel, 512),
        out_shape=[pltpu.VMEM((rows, half), F32), pltpu.VMEM((rows, half), BF16)],
        in_specs=[VMEM_SPEC] * 2,
        out_specs=[VMEM_SPEC] * 2,
        compiler_params=pltpu.CompilerParams(vmem_limit_bytes=4 * 2**20),
        name="down",
    )(in_vmem(act), in_vmem(down))


def shards(tokens, expert_ids, gate_weights, w_gate, w_up, w_down):
    experts = lax.axis_size("expert")
    local_rows, half = tokens.shape
    x00 = jnp.concatenate([tokens] + [shift(tokens, "expert", d) for d in range(1, experts)], axis=0)
    gate_v = load(w_gate[0], tokens)
    x00, gate_v = lax.optimization_barrier((x00, gate_v))
    x01 = shift(x00, "hidden", 1)
    up_v = load(w_up[0], x00)
    x01, up_v = lax.optimization_barrier((x01, up_v))
    x10 = shift(x00, "request", 1)
    x11 = shift(x01, "request", 1)
    act, down_mine, keep_other, send_other = hidden_part(x00, x01, x10, x11, gate_v, up_v, w_down[0])
    got_other = shift(send_other, "request", 1)
    keep_mine, send_mine = down_part(act, down_mine)
    sum_other = (keep_other + got_other.astype(F32)).astype(BF16)
    from_hidden = shift(sum_other, "hidden", 1)
    got_mine = shift(send_mine, "request", 1)
    sum_mine = keep_mine + got_mine.astype(F32)
    out = (sum_mine + from_hidden.astype(F32)).astype(BF16).reshape(experts, local_rows, half)
    me = lax.axis_index("expert")
    combined = jnp.zeros((local_rows, half), F32)
    for d in range(experts):
        rows = out[d] if d == 0 else shift(out[d], "expert", -d)
        chosen = expert_ids == (me + d) % experts
        weight = jnp.sum(jnp.where(chosen, gate_weights, 0.0), axis=1, keepdims=True)
        combined = combined + weight * rows.astype(F32)
    return combined.astype(BF16)


def shards_any(tokens, expert_ids, gate_weights, w_gate, w_up, w_down):
    experts, requests, slices = (lax.axis_size(a) for a in ("expert", "request", "hidden"))
    local_rows, width = tokens.shape
    rows = lax.all_gather(tokens, "hidden", axis=1, tiled=True)
    rows = lax.all_gather(rows, ("expert", "request"), axis=0, tiled=True)
    gate = jnp.dot(rows, w_gate[0], preferred_element_type=F32)
    up = jnp.dot(rows, w_up[0], preferred_element_type=F32)
    act = (jax.nn.silu(gate) * up).astype(BF16)
    out = jnp.dot(act, w_down[0], preferred_element_type=F32)
    out = out.reshape(experts, requests, local_rows, slices, width)
    out = out.transpose(3, 1, 0, 2, 4).reshape(slices * requests, experts * local_rows, width)
    out = lax.psum_scatter(out, ("hidden", "request"), scatter_dimension=0, tiled=True)
    out = out.reshape(experts, local_rows, width).astype(BF16)
    out = lax.all_to_all(out, "expert", split_axis=0, concat_axis=0, tiled=True)
    chosen = expert_ids[:, :, None] == jnp.arange(experts, dtype=jnp.int32)
    weights = jnp.sum(jnp.where(chosen, gate_weights[:, :, None], 0.0), axis=1)
    combined = jnp.sum(weights.T[:, :, None] * out.astype(F32), axis=0)
    return combined.astype(BF16)


def solution(mesh):
    halves = mesh.shape["hidden"] == 2 and mesh.shape["request"] == 2
    return jax.shard_map(
        shards if halves else shards_any,
        mesh=mesh,
        in_specs=(
            P(("replica", "expert", "request"), "hidden"),
            P(("replica", "expert", "request"), None),
            P(("replica", "expert", "request"), None),
            P("expert", None, ("hidden", "request")),
            P("expert", None, ("hidden", "request")),
            P("expert", ("hidden", "request"), None),
        ),
        out_specs=P(("replica", "expert", "request"), "hidden"),
        check_vma=False,
    )
```

```python
import functools

import jax
import jax.numpy as jnp
from jax import lax
from jax.experimental import pallas as pl
from jax.experimental.pallas import tpu as pltpu
from jax.sharding import PartitionSpec as P

F32 = jnp.float32
BF16 = jnp.bfloat16
VMEM_SPEC = pl.BlockSpec(memory_space=pltpu.VMEM)
HBM_SPEC = pl.BlockSpec(memory_space=pltpu.HBM)


def shift(x, axis, by):
    size = lax.axis_size(axis)
    return lax.ppermute(x, axis, [(i, (i + by) % size) for i in range(size)])


def in_hbm(x):
    return pltpu.with_memory_space_constraint(x, pltpu.HBM)


def in_vmem(x):
    return pltpu.with_memory_space_constraint(x, pltpu.VMEM)


def half_copy(hbm, part, cols, dst, sem):
    mine = lax.axis_index("hidden")
    half = hbm.shape[0] // 2
    start = pl.multiple_of((mine if part == 0 else 1 - mine) * half, half)
    return pltpu.make_async_copy(hbm.at[pl.ds(start, half), cols], dst, sem)


def load_kernel(held, gate_hbm, up_hbm, gate_ref, up_ref, sems):
    first = slice(0, held)
    copies = [
        half_copy(gate_hbm, 0, slice(None), gate_ref, sems.at[0]),
        half_copy(up_hbm, 0, first, up_ref.at[:, first], sems.at[1]),
    ]
    for copy in copies:
        copy.start()
    for copy in copies:
        copy.wait()


def load_part(gate, up, held):
    return pl.pallas_call(
        functools.partial(load_kernel, held),
        out_shape=[pltpu.VMEM((gate.shape[0] // 2, gate.shape[1]), BF16)] * 2,
        in_specs=[HBM_SPEC] * 2,
        out_specs=[VMEM_SPEC] * 2,
        scratch_shapes=[pltpu.SemaphoreType.DMA((2,))],
        compiler_params=pltpu.CompilerParams(vmem_limit_bytes=2**20),
        name="load",
    )(in_hbm(gate), in_hbm(up))


def column_block(j, block):
    return pl.ds(pl.multiple_of(j * block, block), block)


def first_kernel(
    block, held, x0, x1, gate_ref, up_in, gate_hbm, up_hbm,
    gate_sum, up_sum, gate_next, up_next, up_ref, x_ref, sems,
):
    rows = x0.shape[0]
    rest = slice(held, None)
    early = half_copy(up_hbm, 0, rest, up_ref.at[:, rest], sems.at[0])
    late = [
        half_copy(gate_hbm, 1, slice(None), gate_next, sems.at[1]),
        half_copy(up_hbm, 1, slice(None), up_next, sems.at[2]),
    ]
    for copy in [early] + late:
        copy.start()
    x_ref[0:rows] = x0[...]
    x_ref[rows:] = x1[...]

    @pl.loop(0, gate_ref.shape[1] // block)
    def _(j):
        @pl.when(j == held // block)
        def _():
            early.wait()

        s = column_block(j, block)
        gate_sum[:, s] = jnp.dot(x_ref[...], gate_ref[:, s], preferred_element_type=F32)
        up_sum[:, s] = jnp.dot(x_ref[...], up_ref[:, s], preferred_element_type=F32)

    for copy in late:
        copy.wait()


def first_part(x0, x1, gate_v, up_v, gate, up, block, held):
    rows, half = x0.shape
    ff = gate.shape[1]
    out = pl.pallas_call(
        functools.partial(first_kernel, block, held),
        out_shape=[pltpu.VMEM((2 * rows, ff), F32)] * 2 + [pltpu.VMEM((half, ff), BF16)] * 3,
        in_specs=[VMEM_SPEC] * 4 + [HBM_SPEC] * 2,
        out_specs=[VMEM_SPEC] * 5,
        scratch_shapes=[
            pltpu.VMEM((2 * rows, half), BF16),
            pltpu.SemaphoreType.DMA((3,)),
        ],
        input_output_aliases={3: 4},
        compiler_params=pltpu.CompilerParams(vmem_limit_bytes=4 * 2**20),
        name="first",
    )(x0, x1, in_vmem(gate_v), in_vmem(up_v), in_hbm(gate), in_hbm(up))
    return out[:4]


def hidden_kernel(
    block, down_block, x0, x1, gate_sum, up_sum, gate_ref, up_ref, down_hbm,
    act_ref, keep_ref, send_ref, x_ref, down_ref, sems,
):
    mine = lax.axis_index("hidden")
    rows, half = x0.shape

    def copy(j):
        start = pl.multiple_of((1 - mine) * half + j * down_block, 128)
        return pltpu.make_async_copy(
            down_hbm.at[:, pl.ds(start, down_block)],
            down_ref.at[:, column_block(j, down_block)],
            sems.at[j],
        )

    for j in range(half // down_block):
        copy(j).start()
    x_ref[0:rows] = x0[...]
    x_ref[rows:] = x1[...]

    @pl.loop(0, gate_ref.shape[1] // block)
    def _(j):
        s = column_block(j, block)
        gate = gate_sum[:, s] + jnp.dot(x_ref[...], gate_ref[:, s], preferred_element_type=F32)
        up = up_sum[:, s] + jnp.dot(x_ref[...], up_ref[:, s], preferred_element_type=F32)
        act_ref[:, s] = (gate / (1.0 + jnp.exp(-gate)) * up).astype(BF16)

    @pl.loop(0, half // down_block)
    def _(j):
        copy(j).wait()
        s = column_block(j, down_block)
        out = jnp.dot(act_ref[...], down_ref[:, s], preferred_element_type=F32)
        keep_ref[:, s] = out[:rows]
        send_ref[:, s] = out[rows:].astype(BF16)


def hidden_part(x0, x1, gate_sum, up_sum, gate_v, up_v, down, block, down_block):
    rows, half = x0.shape
    ff = down.shape[0]
    return pl.pallas_call(
        functools.partial(hidden_kernel, block, down_block),
        out_shape=[
            pltpu.VMEM((2 * rows, ff), BF16),
            pltpu.VMEM((rows, half), F32),
            pltpu.VMEM((rows, half), BF16),
        ],
        in_specs=[VMEM_SPEC] * 6 + [HBM_SPEC],
        out_specs=[VMEM_SPEC] * 3,
        scratch_shapes=[
            pltpu.VMEM((2 * rows, half), BF16),
            pltpu.VMEM((ff, half), BF16),
            pltpu.SemaphoreType.DMA((half // down_block,)),
        ],
        compiler_params=pltpu.CompilerParams(vmem_limit_bytes=12 * 2**20),
        name="hidden",
    )(
        x0, x1, in_vmem(gate_sum), in_vmem(up_sum), in_vmem(gate_v), in_vmem(up_v), in_hbm(down)
    )


def down_kernel(block, act_ref, down_hbm, keep_ref, send_ref, down_ref, sems):
    mine = lax.axis_index("hidden")
    rows, half = keep_ref.shape

    def copy(j):
        start = pl.multiple_of(mine * half + j * block, 128)
        return pltpu.make_async_copy(
            down_hbm.at[:, pl.ds(start, block)],
            down_ref.at[:, column_block(j, block)],
            sems.at[j],
        )

    for j in range(half // block):
        copy(j).start()

    @pl.loop(0, half // block)
    def _(j):
        copy(j).wait()
        s = column_block(j, block)
        out = jnp.dot(act_ref[...], down_ref[:, s], preferred_element_type=F32)
        keep_ref[:, s] = out[:rows]
        send_ref[:, s] = out[rows:].astype(BF16)


def down_part(act, down, half):
    rows, ff = act.shape[0] // 2, down.shape[0]
    block = half // 3
    return pl.pallas_call(
        functools.partial(down_kernel, block),
        out_shape=[pltpu.VMEM((rows, half), F32), pltpu.VMEM((rows, half), BF16)],
        in_specs=[VMEM_SPEC, HBM_SPEC],
        out_specs=[VMEM_SPEC] * 2,
        scratch_shapes=[
            pltpu.VMEM((ff, half), BF16),
            pltpu.SemaphoreType.DMA((half // block,)),
        ],
        compiler_params=pltpu.CompilerParams(vmem_limit_bytes=10 * 2**20),
        name="down",
    )(in_vmem(act), in_hbm(down))


def shards(tokens, expert_ids, gate_weights, w_gate, w_up, w_down):
    experts = lax.axis_size("expert")
    local_rows, half = tokens.shape
    gate, up, down = w_gate[0], w_up[0], w_down[0]
    block = gate.shape[1] // 4
    x00 = jnp.concatenate([tokens] + [shift(tokens, "expert", d) for d in range(1, experts)], axis=0)
    gate_v, up_v = load_part(gate, up, 3 * block)
    x00, gate_v, up_v = lax.optimization_barrier((x00, gate_v, up_v))
    x10 = shift(x00, "request", 1)
    x01 = shift(x00, "hidden", 1)
    gate_sum, up_sum, gate_v, up_v = first_part(
        x00, x10, gate_v, up_v, gate, up, 2 * block, 3 * block
    )
    x01, gate_sum = lax.optimization_barrier((x01, gate_sum))
    x11 = shift(x01, "request", 1)
    act, keep_other, send_other = hidden_part(
        x01, x11, gate_sum, up_sum, gate_v, up_v, down, 2 * block, half // 2
    )
    got_other = shift(send_other, "request", 1)
    sum_other = (keep_other + got_other.astype(F32)).astype(BF16)
    sum_other, act = lax.optimization_barrier((sum_other, act))
    from_hidden = shift(sum_other, "hidden", 1)
    keep_mine, send_mine = down_part(act, down, half)
    got_mine = shift(send_mine, "request", 1)
    sum_mine = lax.optimization_barrier(keep_mine + from_hidden.astype(F32))
    out = (sum_mine + got_mine.astype(F32)).astype(BF16).reshape(experts, local_rows, half)
    me = lax.axis_index("expert")
    combined = jnp.zeros((local_rows, half), F32)
    for d in range(experts):
        rows = out[d] if d == 0 else shift(out[d], "expert", -d)
        chosen = expert_ids == (me + d) % experts
        weight = jnp.sum(jnp.where(chosen, gate_weights, 0.0), axis=1, keepdims=True)
        combined = combined + weight * rows.astype(F32)
    return combined.astype(BF16)


def shards_any(tokens, expert_ids, gate_weights, w_gate, w_up, w_down):
    experts, requests, slices = (lax.axis_size(a) for a in ("expert", "request", "hidden"))
    local_rows, width = tokens.shape
    rows = lax.all_gather(tokens, "hidden", axis=1, tiled=True)
    rows = lax.all_gather(rows, ("expert", "request"), axis=0, tiled=True)
    gate = jnp.dot(rows, w_gate[0], preferred_element_type=F32)
    up = jnp.dot(rows, w_up[0], preferred_element_type=F32)
    act = (jax.nn.silu(gate) * up).astype(BF16)
    out = jnp.dot(act, w_down[0], preferred_element_type=F32)
    out = out.reshape(experts, requests, local_rows, slices, width)
    out = out.transpose(3, 1, 0, 2, 4).reshape(slices * requests, experts * local_rows, width)
    out = lax.psum_scatter(out, ("hidden", "request"), scatter_dimension=0, tiled=True)
    out = out.reshape(experts, local_rows, width).astype(BF16)
    out = lax.all_to_all(out, "expert", split_axis=0, concat_axis=0, tiled=True)
    chosen = expert_ids[:, :, None] == jnp.arange(experts, dtype=jnp.int32)
    weights = jnp.sum(jnp.where(chosen, gate_weights[:, :, None], 0.0), axis=1)
    combined = jnp.sum(weights.T[:, :, None] * out.astype(F32), axis=0)
    return combined.astype(BF16)


def solution(mesh):
    halves = mesh.shape["hidden"] == 2 and mesh.shape["request"] == 2
    return jax.shard_map(
        shards if halves else shards_any,
        mesh=mesh,
        in_specs=(
            P(("replica", "expert", "request"), "hidden"),
            P(("replica", "expert", "request"), None),
            P(("replica", "expert", "request"), None),
            P("expert", None, ("hidden", "request")),
            P("expert", None, ("hidden", "request")),
            P("expert", ("hidden", "request"), None),
        ),
        out_specs=P(("replica", "expert", "request"), "hidden"),
        check_vma=False,
    )
```

```python
import functools

import jax
import jax.numpy as jnp
from jax import lax
from jax.experimental import pallas as pl
from jax.experimental.pallas import tpu as pltpu
from jax.sharding import PartitionSpec as P

F32 = jnp.float32
BF16 = jnp.bfloat16
VMEM_SPEC = pl.BlockSpec(memory_space=pltpu.VMEM)
HBM_SPEC = pl.BlockSpec(memory_space=pltpu.HBM)


def shift(x, axis, by):
    size = lax.axis_size(axis)
    return lax.ppermute(x, axis, [(i, (i + by) % size) for i in range(size)])


def in_hbm(x):
    return pltpu.with_memory_space_constraint(x, pltpu.HBM)


def in_vmem(x):
    return pltpu.with_memory_space_constraint(x, pltpu.VMEM)


def half_copy(hbm, part, cols, dst, sem):
    mine = lax.axis_index("hidden")
    half = hbm.shape[0] // 2
    start = pl.multiple_of((mine if part == 0 else 1 - mine) * half, half)
    return pltpu.make_async_copy(hbm.at[pl.ds(start, half), cols], dst, sem)


def load_kernel(held, gate_hbm, up_hbm, gate_ref, up_ref, sems):
    first = slice(0, held)
    copies = [
        half_copy(gate_hbm, 0, slice(None), gate_ref, sems.at[0]),
        half_copy(up_hbm, 0, first, up_ref.at[:, first], sems.at[1]),
    ]
    for copy in copies:
        copy.start()
    for copy in copies:
        copy.wait()


def load_part(gate, up, held):
    return pl.pallas_call(
        functools.partial(load_kernel, held),
        out_shape=[pltpu.VMEM((gate.shape[0] // 2, gate.shape[1]), BF16)] * 2,
        in_specs=[HBM_SPEC] * 2,
        out_specs=[VMEM_SPEC] * 2,
        scratch_shapes=[pltpu.SemaphoreType.DMA((2,))],
        compiler_params=pltpu.CompilerParams(vmem_limit_bytes=2**20),
        name="load",
    )(in_hbm(gate), in_hbm(up))


def column_block(j, block):
    return pl.ds(pl.multiple_of(j * block, block), block)


def first_kernel(
    block, held, x0, x1, gate_ref, up_in, gate_hbm, up_hbm,
    gate_sum, up_sum, gate_next, up_next, up_ref, x_ref, sems,
):
    rows = x0.shape[0]
    rest = slice(held, None)
    early = half_copy(up_hbm, 0, rest, up_ref.at[:, rest], sems.at[0])
    late = [
        half_copy(gate_hbm, 1, slice(None), gate_next, sems.at[1]),
        half_copy(up_hbm, 1, slice(None), up_next, sems.at[2]),
    ]
    for copy in [early] + late:
        copy.start()
    x_ref[0:rows] = x0[...]
    x_ref[rows:] = x1[...]

    @pl.loop(0, gate_ref.shape[1] // block)
    def _(j):
        @pl.when(j == held // block)
        def _():
            early.wait()

        s = column_block(j, block)
        gate_sum[:, s] = jnp.dot(x_ref[...], gate_ref[:, s], preferred_element_type=F32)
        up_sum[:, s] = jnp.dot(x_ref[...], up_ref[:, s], preferred_element_type=F32)

    for copy in late:
        copy.wait()


def first_part(x0, x1, gate_v, up_v, gate, up, block, held):
    rows, half = x0.shape
    ff = gate.shape[1]
    out = pl.pallas_call(
        functools.partial(first_kernel, block, held),
        out_shape=[pltpu.VMEM((2 * rows, ff), F32)] * 2 + [pltpu.VMEM((half, ff), BF16)] * 3,
        in_specs=[VMEM_SPEC] * 4 + [HBM_SPEC] * 2,
        out_specs=[VMEM_SPEC] * 5,
        scratch_shapes=[
            pltpu.VMEM((2 * rows, half), BF16),
            pltpu.SemaphoreType.DMA((3,)),
        ],
        input_output_aliases={3: 4},
        compiler_params=pltpu.CompilerParams(vmem_limit_bytes=4 * 2**20),
        name="first",
    )(x0, x1, in_vmem(gate_v), in_vmem(up_v), in_hbm(gate), in_hbm(up))
    return out[:4]


def down_copies(hbm, part, block, first, dst, sems):
    mine = lax.axis_index("hidden")
    half = hbm.shape[1] // 2

    def copy(j):
        start = pl.multiple_of((mine if part == 0 else 1 - mine) * half + j * block, 128)
        return pltpu.make_async_copy(
            hbm.at[:, pl.ds(start, block)], dst.at[:, column_block(j - first, block)], sems.at[j]
        )

    return copy


def down_block(act_ref, down_cols, keep_ref, send_ref, s):
    rows = keep_ref.shape[0]
    out = jnp.dot(act_ref[...], down_cols, preferred_element_type=F32)
    keep_ref[:, s] = out[:rows]
    send_ref[:, s] = out[rows:].astype(BF16)


def hidden_kernel(
    block, other_block, mine_block, x0, x1, gate_sum, up_sum, gate_ref, up_ref, down_hbm,
    act_ref, keep_ref, send_ref, mine_ref, x_ref, other_ref, other_sems, mine_sems,
):
    rows, half = x0.shape
    other = down_copies(down_hbm, 1, other_block, 0, other_ref, other_sems)
    mine = down_copies(down_hbm, 0, mine_block, 0, mine_ref, mine_sems)
    for j in range(half // other_block):
        other(j).start()
    x_ref[0:rows] = x0[...]
    x_ref[rows:] = x1[...]

    @pl.loop(0, gate_ref.shape[1] // block)
    def _(j):
        s = column_block(j, block)
        gate = gate_sum[:, s] + jnp.dot(x_ref[...], gate_ref[:, s], preferred_element_type=F32)
        up = up_sum[:, s] + jnp.dot(x_ref[...], up_ref[:, s], preferred_element_type=F32)
        act_ref[:, s] = (gate / (1.0 + jnp.exp(-gate)) * up).astype(BF16)

    mine(0).start()

    @pl.loop(0, half // other_block)
    def _(j):
        other(j).wait()
        s = column_block(j, other_block)
        down_block(act_ref, other_ref[:, s], keep_ref, send_ref, s)

    mine(0).wait()


def hidden_part(x0, x1, gate_sum, up_sum, gate_v, up_v, down, block, other_block, mine_block):
    rows, half = x0.shape
    ff = down.shape[0]
    return pl.pallas_call(
        functools.partial(hidden_kernel, block, other_block, mine_block),
        out_shape=[
            pltpu.VMEM((2 * rows, ff), BF16),
            pltpu.VMEM((rows, half), F32),
            pltpu.VMEM((rows, half), BF16),
            pltpu.VMEM((ff, mine_block), BF16),
        ],
        in_specs=[VMEM_SPEC] * 6 + [HBM_SPEC],
        out_specs=[VMEM_SPEC] * 4,
        scratch_shapes=[
            pltpu.VMEM((2 * rows, half), BF16),
            pltpu.VMEM((ff, half), BF16),
            pltpu.SemaphoreType.DMA((half // other_block,)),
            pltpu.SemaphoreType.DMA((1,)),
        ],
        compiler_params=pltpu.CompilerParams(vmem_limit_bytes=12 * 2**20),
        name="hidden",
    )(
        x0, x1, in_vmem(gate_sum), in_vmem(up_sum), in_vmem(gate_v), in_vmem(up_v), in_hbm(down)
    )


def down_kernel(act_ref, first_ref, down_hbm, keep_ref, send_ref, rest_ref, sems):
    block = first_ref.shape[1]
    blocks = keep_ref.shape[1] // block
    copy = down_copies(down_hbm, 0, block, 1, rest_ref, sems)
    for j in range(1, blocks):
        copy(j).start()
    down_block(act_ref, first_ref[...], keep_ref, send_ref, slice(0, block))

    @pl.loop(1, blocks)
    def _(j):
        copy(j).wait()
        rest = rest_ref[:, column_block(j - 1, block)]
        down_block(act_ref, rest, keep_ref, send_ref, column_block(j, block))


def down_part(act, down_v, down, half):
    rows, ff = act.shape[0] // 2, act.shape[1]
    block = down_v.shape[1]
    return pl.pallas_call(
        down_kernel,
        out_shape=[pltpu.VMEM((rows, half), F32), pltpu.VMEM((rows, half), BF16)],
        in_specs=[VMEM_SPEC, VMEM_SPEC, HBM_SPEC],
        out_specs=[VMEM_SPEC] * 2,
        scratch_shapes=[
            pltpu.VMEM((ff, half - block), BF16),
            pltpu.SemaphoreType.DMA((half // block,)),
        ],
        compiler_params=pltpu.CompilerParams(vmem_limit_bytes=8 * 2**20),
        name="down",
    )(in_vmem(act), in_vmem(down_v), in_hbm(down))


def shards(tokens, expert_ids, gate_weights, w_gate, w_up, w_down):
    experts = lax.axis_size("expert")
    local_rows, half = tokens.shape
    gate, up, down = w_gate[0], w_up[0], w_down[0]
    block = gate.shape[1] // 4
    x00 = jnp.concatenate([tokens] + [shift(tokens, "expert", d) for d in range(1, experts)], axis=0)
    gate_v, up_v = load_part(gate, up, 3 * block)
    x00, gate_v, up_v = lax.optimization_barrier((x00, gate_v, up_v))
    x10 = shift(x00, "request", 1)
    x01 = shift(x00, "hidden", 1)
    gate_sum, up_sum, gate_v, up_v = first_part(
        x00, x10, gate_v, up_v, gate, up, 2 * block, 3 * block
    )
    x01, gate_sum = lax.optimization_barrier((x01, gate_sum))
    x11 = shift(x01, "request", 1)
    act, keep_other, send_other, down_v = hidden_part(
        x01, x11, gate_sum, up_sum, gate_v, up_v, down, 2 * block, half // 2, half // 3
    )
    got_other = shift(send_other, "request", 1)
    sum_other = (keep_other + got_other.astype(F32)).astype(BF16)
    sum_other, act = lax.optimization_barrier((sum_other, act))
    from_hidden = shift(sum_other[local_rows:], "hidden", 1)
    keep_mine, send_mine = down_part(act, down_v, down, half)
    own_other, keep_mine = lax.optimization_barrier((sum_other[:local_rows], keep_mine))
    own_from_hidden = shift(own_other, "hidden", 1)
    got_mine = shift(send_mine, "request", 1).astype(F32)
    away = lax.optimization_barrier(keep_mine[local_rows:] + from_hidden.astype(F32))
    away = (away + got_mine[local_rows:]).astype(BF16).reshape(experts - 1, local_rows, half)
    own = keep_mine[:local_rows] + got_mine[:local_rows] + own_from_hidden.astype(F32)
    me = lax.axis_index("expert")
    combined = jnp.zeros((local_rows, half), F32)
    for d in (0, *range(2, experts), 1):
        rows = own.astype(BF16) if d == 0 else shift(away[d - 1], "expert", -d)
        chosen = expert_ids == (me + d) % experts
        weight = jnp.sum(jnp.where(chosen, gate_weights, 0.0), axis=1, keepdims=True)
        combined = combined + weight * rows.astype(F32)
    return combined.astype(BF16)


def shards_any(tokens, expert_ids, gate_weights, w_gate, w_up, w_down):
    experts, requests, slices = (lax.axis_size(a) for a in ("expert", "request", "hidden"))
    local_rows, width = tokens.shape
    rows = lax.all_gather(tokens, "hidden", axis=1, tiled=True)
    rows = lax.all_gather(rows, ("expert", "request"), axis=0, tiled=True)
    gate = jnp.dot(rows, w_gate[0], preferred_element_type=F32)
    up = jnp.dot(rows, w_up[0], preferred_element_type=F32)
    act = (jax.nn.silu(gate) * up).astype(BF16)
    out = jnp.dot(act, w_down[0], preferred_element_type=F32)
    out = out.reshape(experts, requests, local_rows, slices, width)
    out = out.transpose(3, 1, 0, 2, 4).reshape(slices * requests, experts * local_rows, width)
    out = lax.psum_scatter(out, ("hidden", "request"), scatter_dimension=0, tiled=True)
    out = out.reshape(experts, local_rows, width).astype(BF16)
    out = lax.all_to_all(out, "expert", split_axis=0, concat_axis=0, tiled=True)
    chosen = expert_ids[:, :, None] == jnp.arange(experts, dtype=jnp.int32)
    weights = jnp.sum(jnp.where(chosen, gate_weights[:, :, None], 0.0), axis=1)
    combined = jnp.sum(weights.T[:, :, None] * out.astype(F32), axis=0)
    return combined.astype(BF16)


def solution(mesh):
    halves = mesh.shape["hidden"] == 2 and mesh.shape["request"] == 2
    return jax.shard_map(
        shards if halves else shards_any,
        mesh=mesh,
        in_specs=(
            P(("replica", "expert", "request"), "hidden"),
            P(("replica", "expert", "request"), None),
            P(("replica", "expert", "request"), None),
            P("expert", None, ("hidden", "request")),
            P("expert", None, ("hidden", "request")),
            P("expert", ("hidden", "request"), None),
        ),
        out_specs=P(("replica", "expert", "request"), "hidden"),
        check_vma=False,
    )
```

```python
import functools

import jax
import jax.numpy as jnp
from jax import lax
from jax.experimental import pallas as pl
from jax.experimental.pallas import tpu as pltpu
from jax.sharding import PartitionSpec as P

F32 = jnp.float32
BF16 = jnp.bfloat16
VMEM_SPEC = pl.BlockSpec(memory_space=pltpu.VMEM)
HBM_SPEC = pl.BlockSpec(memory_space=pltpu.HBM)


def shift(x, axis, by):
    size = lax.axis_size(axis)
    return lax.ppermute(x, axis, [(i, (i + by) % size) for i in range(size)])


def in_hbm(x):
    return pltpu.with_memory_space_constraint(x, pltpu.HBM)


def in_vmem(x):
    return pltpu.with_memory_space_constraint(x, pltpu.VMEM)


def half_copy(hbm, part, cols, dst, sem):
    mine = lax.axis_index("hidden")
    half = hbm.shape[0] // 2
    start = pl.multiple_of((mine if part == 0 else 1 - mine) * half, half)
    return pltpu.make_async_copy(hbm.at[pl.ds(start, half), cols], dst, sem)


def load_kernel(held, gate_hbm, up_hbm, gate_ref, up_ref, sems):
    first = slice(0, held)
    copies = [
        half_copy(gate_hbm, 0, slice(None), gate_ref, sems.at[0]),
        half_copy(up_hbm, 0, first, up_ref.at[:, first], sems.at[1]),
    ]
    for copy in copies:
        copy.start()
    for copy in copies:
        copy.wait()


def load_part(gate, up, held):
    return pl.pallas_call(
        functools.partial(load_kernel, held),
        out_shape=[pltpu.VMEM((gate.shape[0] // 2, gate.shape[1]), BF16)] * 2,
        in_specs=[HBM_SPEC] * 2,
        out_specs=[VMEM_SPEC] * 2,
        scratch_shapes=[pltpu.SemaphoreType.DMA((2,))],
        compiler_params=pltpu.CompilerParams(vmem_limit_bytes=2**20),
        name="load",
    )(in_hbm(gate), in_hbm(up))


def column_block(j, block):
    return pl.ds(pl.multiple_of(j * block, block), block)


def down_copies(hbm, part, block, first, dst, sems):
    mine = lax.axis_index("hidden")
    half = hbm.shape[1] // 2

    def copy(j):
        start = pl.multiple_of((mine if part == 0 else 1 - mine) * half + j * block, 128)
        return pltpu.make_async_copy(
            hbm.at[:, pl.ds(start, block)], dst.at[:, column_block(j - first, block)], sems.at[j]
        )

    return copy


def down_block(act_ref, down_cols, keep_ref, send_ref, s):
    rows = keep_ref.shape[0]
    out = jnp.dot(act_ref[...], down_cols, preferred_element_type=F32)
    keep_ref[:, s] = out[:rows]
    send_ref[:, s] = out[rows:].astype(BF16)


def first_kernel(
    block, held, x0, x1, gate_ref, up_in, gate_hbm, up_hbm, down_hbm,
    gate_sum, up_sum, gate_next, up_next, down_next, up_ref, x_ref, sems, down_sems,
):
    rows = x0.shape[0]
    rest = slice(held, None)
    early = half_copy(up_hbm, 0, rest, up_ref.at[:, rest], sems.at[0])
    late = [
        half_copy(gate_hbm, 1, slice(None), gate_next, sems.at[1]),
        half_copy(up_hbm, 1, slice(None), up_next, sems.at[2]),
        down_copies(down_hbm, 0, down_next.shape[1], 0, down_next, down_sems)(0),
    ]
    for copy in [early] + late:
        copy.start()
    x_ref[0:rows] = x0[...]
    x_ref[rows:] = x1[...]

    @pl.loop(0, gate_ref.shape[1] // block)
    def _(j):
        @pl.when(j == held // block)
        def _():
            early.wait()

        s = column_block(j, block)
        gate_sum[:, s] = jnp.dot(x_ref[...], gate_ref[:, s], preferred_element_type=F32)
        up_sum[:, s] = jnp.dot(x_ref[...], up_ref[:, s], preferred_element_type=F32)

    for copy in late:
        copy.wait()


def first_part(x0, x1, gate_v, up_v, gate, up, down, block, held, mine_block):
    rows, half = x0.shape
    ff = gate.shape[1]
    out = pl.pallas_call(
        functools.partial(first_kernel, block, held),
        out_shape=[pltpu.VMEM((2 * rows, ff), F32)] * 2
        + [pltpu.VMEM((half, ff), BF16)] * 2
        + [pltpu.VMEM((ff, mine_block), BF16), pltpu.VMEM((half, ff), BF16)],
        in_specs=[VMEM_SPEC] * 4 + [HBM_SPEC] * 3,
        out_specs=[VMEM_SPEC] * 6,
        scratch_shapes=[
            pltpu.VMEM((2 * rows, half), BF16),
            pltpu.SemaphoreType.DMA((3,)),
            pltpu.SemaphoreType.DMA((1,)),
        ],
        input_output_aliases={3: 5},
        compiler_params=pltpu.CompilerParams(vmem_limit_bytes=4 * 2**20),
        name="first",
    )(x0, x1, in_vmem(gate_v), in_vmem(up_v), in_hbm(gate), in_hbm(up), in_hbm(down))
    return out[:5]


def hidden_kernel(
    block, other_block, mine_block, x0, x1, gate_sum, up_sum, gate_ref, up_ref, down_hbm,
    act_ref, keep_ref, send_ref, mine_ref, x_ref, other_ref, other_sems, mine_sems,
):
    rows, half = x0.shape
    other = down_copies(down_hbm, 1, other_block, 0, other_ref, other_sems)
    mine = down_copies(down_hbm, 0, mine_block, 1, mine_ref, mine_sems)
    for j in range(half // other_block):
        other(j).start()
    x_ref[0:rows] = x0[...]
    x_ref[rows:] = x1[...]

    @pl.loop(0, gate_ref.shape[1] // block)
    def _(j):
        s = column_block(j, block)
        gate = gate_sum[:, s] + jnp.dot(x_ref[...], gate_ref[:, s], preferred_element_type=F32)
        up = up_sum[:, s] + jnp.dot(x_ref[...], up_ref[:, s], preferred_element_type=F32)
        act_ref[:, s] = (gate / (1.0 + jnp.exp(-gate)) * up).astype(BF16)

    mine(1).start()

    @pl.loop(0, half // other_block)
    def _(j):
        other(j).wait()
        s = column_block(j, other_block)
        down_block(act_ref, other_ref[:, s], keep_ref, send_ref, s)

    mine(1).wait()


def hidden_part(x0, x1, gate_sum, up_sum, gate_v, up_v, down, block, other_block, mine_block):
    rows, half = x0.shape
    ff = down.shape[0]
    return pl.pallas_call(
        functools.partial(hidden_kernel, block, other_block, mine_block),
        out_shape=[
            pltpu.VMEM((2 * rows, ff), BF16),
            pltpu.VMEM((rows, half), F32),
            pltpu.VMEM((rows, half), BF16),
            pltpu.VMEM((ff, mine_block), BF16),
        ],
        in_specs=[VMEM_SPEC] * 6 + [HBM_SPEC],
        out_specs=[VMEM_SPEC] * 4,
        scratch_shapes=[
            pltpu.VMEM((2 * rows, half), BF16),
            pltpu.VMEM((ff, half), BF16),
            pltpu.SemaphoreType.DMA((half // other_block,)),
            pltpu.SemaphoreType.DMA((2,)),
        ],
        compiler_params=pltpu.CompilerParams(vmem_limit_bytes=12 * 2**20),
        name="hidden",
    )(
        x0, x1, in_vmem(gate_sum), in_vmem(up_sum), in_vmem(gate_v), in_vmem(up_v), in_hbm(down)
    )


def down_kernel(act_ref, first_ref, second_ref, down_hbm, keep_ref, send_ref, rest_ref, sems):
    block = first_ref.shape[1]
    copy = down_copies(down_hbm, 0, block, 2, rest_ref, sems)(2)
    copy.start()
    down_block(act_ref, first_ref[...], keep_ref, send_ref, slice(0, block))
    down_block(act_ref, second_ref[...], keep_ref, send_ref, slice(block, 2 * block))
    copy.wait()
    down_block(act_ref, rest_ref[...], keep_ref, send_ref, slice(2 * block, None))


def down_part(act, down_0, down_1, down, half):
    rows, ff = act.shape[0] // 2, act.shape[1]
    return pl.pallas_call(
        down_kernel,
        out_shape=[pltpu.VMEM((rows, half), F32), pltpu.VMEM((rows, half), BF16)],
        in_specs=[VMEM_SPEC] * 3 + [HBM_SPEC],
        out_specs=[VMEM_SPEC] * 2,
        scratch_shapes=[
            pltpu.VMEM((ff, half - 2 * down_0.shape[1]), BF16),
            pltpu.SemaphoreType.DMA((3,)),
        ],
        compiler_params=pltpu.CompilerParams(vmem_limit_bytes=6 * 2**20),
        name="down",
    )(in_vmem(act), in_vmem(down_0), in_vmem(down_1), in_hbm(down))


def combine_kernel(hops, ids_ref, weights_ref, keep_ref, got_ref, hidden_ref, *refs):
    out_ref = refs[-1]
    me = lax.axis_index("expert")
    experts = lax.axis_size("expert")
    rows = out_ref.shape[0]
    ids, weights = ids_ref[...], weights_ref[...]

    def weighted(source, block):
        weight = jnp.sum(jnp.where(ids == source, weights, 0.0), axis=1, keepdims=True)
        return weight * block.astype(F32)

    own = keep_ref[0:rows] + got_ref[0:rows].astype(F32) + hidden_ref[...].astype(F32)
    total = weighted(me, own.astype(BF16))
    for hop, ref in zip(hops, refs[:-1]):
        total = total + weighted(lax.rem(me + hop, experts), ref[...])
    out_ref[...] = total.astype(BF16)


def combine(hops, ids, weights, keep, got, from_hidden, arrived):
    return pl.pallas_call(
        functools.partial(combine_kernel, hops),
        out_shape=jax.ShapeDtypeStruct(from_hidden.shape, BF16),
        in_specs=[VMEM_SPEC] * (5 + len(arrived)),
        out_specs=VMEM_SPEC,
        compiler_params=pltpu.CompilerParams(vmem_limit_bytes=4 * 2**20),
        name="combine",
    )(ids, weights, in_vmem(keep), in_vmem(got), in_vmem(from_hidden), *map(in_vmem, arrived))


def shards(tokens, expert_ids, gate_weights, w_gate, w_up, w_down):
    experts = lax.axis_size("expert")
    local_rows, half = tokens.shape
    gate, up, down = w_gate[0], w_up[0], w_down[0]
    block = gate.shape[1] // 4
    x00 = jnp.concatenate([tokens] + [shift(tokens, "expert", d) for d in range(1, experts)], axis=0)
    gate_v, up_v = load_part(gate, up, 3 * block)
    x00, gate_v, up_v = lax.optimization_barrier((x00, gate_v, up_v))
    x10 = shift(x00, "request", 1)
    x01 = shift(x00, "hidden", 1)
    gate_sum, up_sum, gate_v, up_v, down_0 = first_part(
        x00, x10, gate_v, up_v, gate, up, down, 2 * block, 3 * block, half // 3
    )
    x01, gate_sum = lax.optimization_barrier((x01, gate_sum))
    x11 = shift(x01, "request", 1)
    act, keep_other, send_other, down_1 = hidden_part(
        x01, x11, gate_sum, up_sum, gate_v, up_v, down, 2 * block, half // 2, half // 3
    )
    got_other = shift(send_other, "request", 1)
    sum_other = (keep_other + got_other.astype(F32)).astype(BF16)
    sum_other, act = lax.optimization_barrier((sum_other, act))
    from_hidden = shift(sum_other[local_rows:], "hidden", 1)
    keep_mine, send_mine = down_part(act, down_0, down_1, down, half)
    own_other, keep_mine = lax.optimization_barrier((sum_other[:local_rows], keep_mine))
    own_from_hidden = shift(own_other, "hidden", 1)
    got_mine = shift(send_mine, "request", 1)
    away = lax.optimization_barrier(keep_mine[local_rows:] + from_hidden.astype(F32))
    away = (away + got_mine[local_rows:].astype(F32)).astype(BF16)
    away = away.reshape(experts - 1, local_rows, half)
    hops = (*range(2, experts), 1)
    arrived = [shift(away[d - 1], "expert", -d) for d in hops]
    return combine(
        hops, expert_ids, gate_weights, keep_mine, got_mine, own_from_hidden, arrived
    )


def shards_any(tokens, expert_ids, gate_weights, w_gate, w_up, w_down):
    experts, requests, slices = (lax.axis_size(a) for a in ("expert", "request", "hidden"))
    local_rows, width = tokens.shape
    rows = lax.all_gather(tokens, "hidden", axis=1, tiled=True)
    rows = lax.all_gather(rows, ("expert", "request"), axis=0, tiled=True)
    gate = jnp.dot(rows, w_gate[0], preferred_element_type=F32)
    up = jnp.dot(rows, w_up[0], preferred_element_type=F32)
    act = (jax.nn.silu(gate) * up).astype(BF16)
    out = jnp.dot(act, w_down[0], preferred_element_type=F32)
    out = out.reshape(experts, requests, local_rows, slices, width)
    out = out.transpose(3, 1, 0, 2, 4).reshape(slices * requests, experts * local_rows, width)
    out = lax.psum_scatter(out, ("hidden", "request"), scatter_dimension=0, tiled=True)
    out = out.reshape(experts, local_rows, width).astype(BF16)
    out = lax.all_to_all(out, "expert", split_axis=0, concat_axis=0, tiled=True)
    chosen = expert_ids[:, :, None] == jnp.arange(experts, dtype=jnp.int32)
    weights = jnp.sum(jnp.where(chosen, gate_weights[:, :, None], 0.0), axis=1)
    combined = jnp.sum(weights.T[:, :, None] * out.astype(F32), axis=0)
    return combined.astype(BF16)


def solution(mesh):
    halves = mesh.shape["hidden"] == 2 and mesh.shape["request"] == 2
    return jax.shard_map(
        shards if halves else shards_any,
        mesh=mesh,
        in_specs=(
            P(("replica", "expert", "request"), "hidden"),
            P(("replica", "expert", "request"), None),
            P(("replica", "expert", "request"), None),
            P("expert", None, ("hidden", "request")),
            P("expert", None, ("hidden", "request")),
            P("expert", ("hidden", "request"), None),
        ),
        out_specs=P(("replica", "expert", "request"), "hidden"),
        check_vma=False,
    )
```

```python
import functools

import jax
import jax.numpy as jnp
from jax import lax
from jax.experimental import pallas as pl
from jax.experimental.pallas import tpu as pltpu
from jax.sharding import PartitionSpec as P

F32 = jnp.float32
BF16 = jnp.bfloat16
VMEM_SPEC = pl.BlockSpec(memory_space=pltpu.VMEM)
HBM_SPEC = pl.BlockSpec(memory_space=pltpu.HBM)


def shift(x, axis, by):
    size = lax.axis_size(axis)
    return lax.ppermute(x, axis, [(i, (i + by) % size) for i in range(size)])


def swap(x, by):
    return lax.ppermute(x, "expert", [(i, i ^ by) for i in range(lax.axis_size("expert"))])


def in_hbm(x):
    return pltpu.with_memory_space_constraint(x, pltpu.HBM)


def in_vmem(x):
    return pltpu.with_memory_space_constraint(x, pltpu.VMEM)


def half_copy(hbm, part, cols, dst, sem):
    mine = lax.axis_index("hidden")
    half = hbm.shape[0] // 2
    start = pl.multiple_of((mine if part == 0 else 1 - mine) * half, half)
    return pltpu.make_async_copy(hbm.at[pl.ds(start, half), cols], dst, sem)


def load_kernel(held, gate_hbm, up_hbm, gate_ref, up_ref, sems):
    first = slice(0, held)
    copies = [
        half_copy(gate_hbm, 0, slice(None), gate_ref, sems.at[0]),
        half_copy(up_hbm, 0, first, up_ref.at[:, first], sems.at[1]),
    ]
    for copy in copies:
        copy.start()
    for copy in copies:
        copy.wait()


def load_part(gate, up, held):
    return pl.pallas_call(
        functools.partial(load_kernel, held),
        out_shape=[pltpu.VMEM((gate.shape[0] // 2, gate.shape[1]), BF16)] * 2,
        in_specs=[HBM_SPEC] * 2,
        out_specs=[VMEM_SPEC] * 2,
        scratch_shapes=[pltpu.SemaphoreType.DMA((2,))],
        compiler_params=pltpu.CompilerParams(vmem_limit_bytes=2**20),
        name="load",
    )(in_hbm(gate), in_hbm(up))


def column_block(j, block):
    return pl.ds(pl.multiple_of(j * block, block), block)


def down_copies(hbm, part, block, first, dst, sems):
    mine = lax.axis_index("hidden")
    half = hbm.shape[1] // 2

    def copy(j):
        start = pl.multiple_of((mine if part == 0 else 1 - mine) * half + j * block, 128)
        return pltpu.make_async_copy(
            hbm.at[:, pl.ds(start, block)], dst.at[:, column_block(j - first, block)], sems.at[j]
        )

    return copy


def down_block(act_ref, down_cols, keep_ref, send_ref, s):
    rows = keep_ref.shape[0]
    out = jnp.dot(act_ref[...], down_cols, preferred_element_type=F32)
    keep_ref[:, s] = out[:rows]
    send_ref[:, s] = out[rows:].astype(BF16)


def first_kernel(
    block, held, x0, x1, gate_ref, up_in, gate_hbm, up_hbm, down_hbm,
    gate_sum, up_sum, gate_next, up_next, down_next, up_ref, x_ref, sems, down_sems,
):
    rows = x0.shape[0]
    rest = slice(held, None)
    early = half_copy(up_hbm, 0, rest, up_ref.at[:, rest], sems.at[0])
    late = [
        half_copy(gate_hbm, 1, slice(None), gate_next, sems.at[1]),
        half_copy(up_hbm, 1, slice(None), up_next, sems.at[2]),
        down_copies(down_hbm, 0, down_next.shape[1], 0, down_next, down_sems)(0),
    ]
    for copy in [early] + late:
        copy.start()
    x_ref[0:rows] = x0[...]
    x_ref[rows:] = x1[...]

    @pl.loop(0, gate_ref.shape[1] // block)
    def _(j):
        @pl.when(j == held // block)
        def _():
            early.wait()

        s = column_block(j, block)
        gate_sum[:, s] = jnp.dot(x_ref[...], gate_ref[:, s], preferred_element_type=F32)
        up_sum[:, s] = jnp.dot(x_ref[...], up_ref[:, s], preferred_element_type=F32)

    for copy in late:
        copy.wait()


def first_part(x0, x1, gate_v, up_v, gate, up, down, block, held, mine_block):
    rows, half = x0.shape
    ff = gate.shape[1]
    out = pl.pallas_call(
        functools.partial(first_kernel, block, held),
        out_shape=[pltpu.VMEM((2 * rows, ff), F32)] * 2
        + [pltpu.VMEM((half, ff), BF16)] * 2
        + [pltpu.VMEM((ff, mine_block), BF16), pltpu.VMEM((half, ff), BF16)],
        in_specs=[VMEM_SPEC] * 4 + [HBM_SPEC] * 3,
        out_specs=[VMEM_SPEC] * 6,
        scratch_shapes=[
            pltpu.VMEM((2 * rows, half), BF16),
            pltpu.SemaphoreType.DMA((3,)),
            pltpu.SemaphoreType.DMA((1,)),
        ],
        input_output_aliases={3: 5},
        compiler_params=pltpu.CompilerParams(vmem_limit_bytes=4 * 2**20),
        name="first",
    )(x0, x1, in_vmem(gate_v), in_vmem(up_v), in_hbm(gate), in_hbm(up), in_hbm(down))
    return out[:5]


def hidden_kernel(
    block, other_block, x0, x1, gate_sum, up_sum, gate_ref, up_ref, down_hbm,
    act_ref, keep_ref, send_ref, x_ref, other_ref, sems,
):
    rows, half = x0.shape
    other = down_copies(down_hbm, 1, other_block, 0, other_ref, sems)
    for j in range(half // other_block):
        other(j).start()
    x_ref[0:rows] = x0[...]
    x_ref[rows:] = x1[...]

    @pl.loop(0, gate_ref.shape[1] // block)
    def _(j):
        s = column_block(j, block)
        gate = gate_sum[:, s] + jnp.dot(x_ref[...], gate_ref[:, s], preferred_element_type=F32)
        up = up_sum[:, s] + jnp.dot(x_ref[...], up_ref[:, s], preferred_element_type=F32)
        act_ref[:, s] = (gate / (1.0 + jnp.exp(-gate)) * up).astype(BF16)

    @pl.loop(0, half // other_block)
    def _(j):
        other(j).wait()
        s = column_block(j, other_block)
        down_block(act_ref, other_ref[:, s], keep_ref, send_ref, s)


def hidden_part(x0, x1, gate_sum, up_sum, gate_v, up_v, down, block, other_block):
    rows, half = x0.shape
    ff = down.shape[0]
    return pl.pallas_call(
        functools.partial(hidden_kernel, block, other_block),
        out_shape=[
            pltpu.VMEM((2 * rows, ff), BF16),
            pltpu.VMEM((rows, half), F32),
            pltpu.VMEM((rows, half), BF16),
        ],
        in_specs=[VMEM_SPEC] * 6 + [HBM_SPEC],
        out_specs=[VMEM_SPEC] * 3,
        scratch_shapes=[
            pltpu.VMEM((2 * rows, half), BF16),
            pltpu.VMEM((ff, half), BF16),
            pltpu.SemaphoreType.DMA((half // other_block,)),
        ],
        compiler_params=pltpu.CompilerParams(vmem_limit_bytes=12 * 2**20),
        name="hidden",
    )(
        x0, x1, in_vmem(gate_sum), in_vmem(up_sum), in_vmem(gate_v), in_vmem(up_v), in_hbm(down)
    )


def down_kernel(act_ref, first_ref, down_hbm, keep_ref, send_ref, rest_ref, sems):
    block = first_ref.shape[1]
    blocks = keep_ref.shape[1] // block
    copy = down_copies(down_hbm, 0, block, 1, rest_ref, sems)
    for j in range(1, blocks):
        copy(j).start()
    down_block(act_ref, first_ref[...], keep_ref, send_ref, slice(0, block))

    @pl.loop(1, blocks)
    def _(j):
        copy(j).wait()
        rest = rest_ref[:, column_block(j - 1, block)]
        down_block(act_ref, rest, keep_ref, send_ref, column_block(j, block))


def down_part(act, down_v, down, half):
    rows, ff = act.shape[0] // 2, act.shape[1]
    block = down_v.shape[1]
    return pl.pallas_call(
        down_kernel,
        out_shape=[pltpu.VMEM((rows, half), F32), pltpu.VMEM((rows, half), BF16)],
        in_specs=[VMEM_SPEC, VMEM_SPEC, HBM_SPEC],
        out_specs=[VMEM_SPEC] * 2,
        scratch_shapes=[
            pltpu.VMEM((ff, half - block), BF16),
            pltpu.SemaphoreType.DMA((half // block,)),
        ],
        compiler_params=pltpu.CompilerParams(vmem_limit_bytes=8 * 2**20),
        name="down",
    )(in_vmem(act), in_vmem(down_v), in_hbm(down))


def combine_kernel(swaps, ids_ref, weights_ref, keep_ref, got_ref, hidden_ref, *refs):
    out_ref = refs[-1]
    me = lax.axis_index("expert")
    rows = out_ref.shape[0]
    ids, weights = ids_ref[...], weights_ref[...]

    def weighted(source, block):
        weight = jnp.sum(jnp.where(ids == source, weights, 0.0), axis=1, keepdims=True)
        return weight * block.astype(F32)

    own = keep_ref[0:rows] + got_ref[0:rows].astype(F32) + hidden_ref[...].astype(F32)
    total = weighted(me, own.astype(BF16))
    for by, ref in zip(swaps, refs[:-1]):
        total = total + weighted(me ^ by, ref[...])
    out_ref[...] = total.astype(BF16)


def combine(swaps, ids, weights, keep, got, from_hidden, arrived):
    return pl.pallas_call(
        functools.partial(combine_kernel, swaps),
        out_shape=jax.ShapeDtypeStruct(from_hidden.shape, BF16),
        in_specs=[VMEM_SPEC] * (5 + len(arrived)),
        out_specs=VMEM_SPEC,
        compiler_params=pltpu.CompilerParams(vmem_limit_bytes=4 * 2**20),
        name="combine",
    )(ids, weights, in_vmem(keep), in_vmem(got), in_vmem(from_hidden), *map(in_vmem, arrived))


def shards(tokens, expert_ids, gate_weights, w_gate, w_up, w_down):
    experts = lax.axis_size("expert")
    local_rows, half = tokens.shape
    gate, up, down = w_gate[0], w_up[0], w_down[0]
    block = gate.shape[1] // 4
    swaps = (*range(2, experts), 1)
    x00 = jnp.concatenate([tokens] + [swap(tokens, by) for by in swaps], axis=0)
    gate_v, up_v = load_part(gate, up, 3 * block)
    x00, gate_v, up_v = lax.optimization_barrier((x00, gate_v, up_v))
    x10 = shift(x00, "request", 1)
    x01 = shift(x00, "hidden", 1)
    gate_sum, up_sum, gate_v, up_v, down_0 = first_part(
        x00, x10, gate_v, up_v, gate, up, down, 2 * block, 3 * block, half // 3
    )
    x01, gate_sum = lax.optimization_barrier((x01, gate_sum))
    x11 = shift(x01, "request", 1)
    act, keep_other, send_other = hidden_part(
        x01, x11, gate_sum, up_sum, gate_v, up_v, down, 2 * block, half // 2
    )
    got_other = shift(send_other, "request", 1)
    sum_other = (keep_other + got_other.astype(F32)).astype(BF16)
    sum_other, act = lax.optimization_barrier((sum_other, act))
    from_hidden = shift(sum_other[local_rows:], "hidden", 1)
    keep_mine, send_mine = down_part(act, down_0, down, half)
    own_other, keep_mine = lax.optimization_barrier((sum_other[:local_rows], keep_mine))
    own_from_hidden = shift(own_other, "hidden", 1)
    got_mine = shift(send_mine, "request", 1)
    away = lax.optimization_barrier(keep_mine[local_rows:] + from_hidden.astype(F32))
    away = (away + got_mine[local_rows:].astype(F32)).astype(BF16)
    away = away.reshape(experts - 1, local_rows, half)
    back = tuple(range(experts - 1, 0, -1))
    arrived = [swap(away[swaps.index(by)], by) for by in back]
    return combine(
        back, expert_ids, gate_weights, keep_mine, got_mine, own_from_hidden, arrived
    )


def shards_any(tokens, expert_ids, gate_weights, w_gate, w_up, w_down):
    experts, requests, slices = (lax.axis_size(a) for a in ("expert", "request", "hidden"))
    local_rows, width = tokens.shape
    rows = lax.all_gather(tokens, "hidden", axis=1, tiled=True)
    rows = lax.all_gather(rows, ("expert", "request"), axis=0, tiled=True)
    gate = jnp.dot(rows, w_gate[0], preferred_element_type=F32)
    up = jnp.dot(rows, w_up[0], preferred_element_type=F32)
    act = (jax.nn.silu(gate) * up).astype(BF16)
    out = jnp.dot(act, w_down[0], preferred_element_type=F32)
    out = out.reshape(experts, requests, local_rows, slices, width)
    out = out.transpose(3, 1, 0, 2, 4).reshape(slices * requests, experts * local_rows, width)
    out = lax.psum_scatter(out, ("hidden", "request"), scatter_dimension=0, tiled=True)
    out = out.reshape(experts, local_rows, width).astype(BF16)
    out = lax.all_to_all(out, "expert", split_axis=0, concat_axis=0, tiled=True)
    chosen = expert_ids[:, :, None] == jnp.arange(experts, dtype=jnp.int32)
    weights = jnp.sum(jnp.where(chosen, gate_weights[:, :, None], 0.0), axis=1)
    combined = jnp.sum(weights.T[:, :, None] * out.astype(F32), axis=0)
    return combined.astype(BF16)


def solution(mesh):
    experts = mesh.shape["expert"]
    halves = mesh.shape["hidden"] == 2 and mesh.shape["request"] == 2
    halves = halves and experts & (experts - 1) == 0
    return jax.shard_map(
        shards if halves else shards_any,
        mesh=mesh,
        in_specs=(
            P(("replica", "expert", "request"), "hidden"),
            P(("replica", "expert", "request"), None),
            P(("replica", "expert", "request"), None),
            P("expert", None, ("hidden", "request")),
            P("expert", None, ("hidden", "request")),
            P("expert", ("hidden", "request"), None),
        ),
        out_specs=P(("replica", "expert", "request"), "hidden"),
        check_vma=False,
    )
```

```python
import functools

import jax
import jax.numpy as jnp
from jax import lax
from jax.experimental import pallas as pl
from jax.experimental.pallas import tpu as pltpu
from jax.sharding import PartitionSpec as P

F32 = jnp.float32
BF16 = jnp.bfloat16
VMEM_SPEC = pl.BlockSpec(memory_space=pltpu.VMEM)
HBM_SPEC = pl.BlockSpec(memory_space=pltpu.HBM)


def shift(x, axis, by):
    size = lax.axis_size(axis)
    return lax.ppermute(x, axis, [(i, (i + by) % size) for i in range(size)])


def swap(x, by):
    return lax.ppermute(x, "expert", [(i, i ^ by) for i in range(lax.axis_size("expert"))])


def in_hbm(x):
    return pltpu.with_memory_space_constraint(x, pltpu.HBM)


def in_vmem(x):
    return pltpu.with_memory_space_constraint(x, pltpu.VMEM)


def half_copy(hbm, part, cols, dst, sem):
    mine = lax.axis_index("hidden")
    half = hbm.shape[0] // 2
    start = pl.multiple_of((mine if part == 0 else 1 - mine) * half, half)
    return pltpu.make_async_copy(hbm.at[pl.ds(start, half), cols], dst, sem)


def load_kernel(held, gate_hbm, up_hbm, gate_ref, up_ref, sems):
    first = slice(0, held)
    copies = [
        half_copy(gate_hbm, 0, slice(None), gate_ref, sems.at[0]),
        half_copy(up_hbm, 0, first, up_ref.at[:, first], sems.at[1]),
    ]
    for copy in copies:
        copy.start()
    for copy in copies:
        copy.wait()


def load_part(gate, up, held):
    return pl.pallas_call(
        functools.partial(load_kernel, held),
        out_shape=[pltpu.VMEM((gate.shape[0] // 2, gate.shape[1]), BF16)] * 2,
        in_specs=[HBM_SPEC] * 2,
        out_specs=[VMEM_SPEC] * 2,
        scratch_shapes=[pltpu.SemaphoreType.DMA((2,))],
        compiler_params=pltpu.CompilerParams(vmem_limit_bytes=2**20),
        name="load",
    )(in_hbm(gate), in_hbm(up))


def column_block(j, block):
    return pl.ds(pl.multiple_of(j * block, block), block)


def down_copies(hbm, part, block, first, dst, sems):
    mine = lax.axis_index("hidden")
    half = hbm.shape[1] // 2

    def copy(j):
        start = pl.multiple_of((mine if part == 0 else 1 - mine) * half + j * block, 128)
        return pltpu.make_async_copy(
            hbm.at[:, pl.ds(start, block)], dst.at[:, column_block(j - first, block)], sems.at[j]
        )

    return copy


def down_block(act_ref, down_cols, keep_ref, send_ref, s):
    rows = keep_ref.shape[0]
    out = jnp.dot(act_ref[...], down_cols, preferred_element_type=F32)
    keep_ref[:, s] = out[:rows]
    send_ref[:, s] = out[rows:].astype(BF16)


def first_kernel(
    block, held, x0, x1, gate_ref, up_in, gate_hbm, up_hbm, down_hbm,
    gate_sum, up_sum, gate_next, up_next, down_next, up_ref, x_ref, sems, down_sems,
):
    rows = x0.shape[0]
    rest = slice(held, None)
    early = half_copy(up_hbm, 0, rest, up_ref.at[:, rest], sems.at[0])
    late = [
        half_copy(gate_hbm, 1, slice(None), gate_next, sems.at[1]),
        half_copy(up_hbm, 1, slice(None), up_next, sems.at[2]),
        down_copies(down_hbm, 0, down_next.shape[1], 0, down_next, down_sems)(0),
    ]
    for copy in [early] + late:
        copy.start()
    x_ref[0:rows] = x0[...]
    x_ref[rows:] = x1[...]

    @pl.loop(0, gate_ref.shape[1] // block)
    def _(j):
        @pl.when(j == held // block)
        def _():
            early.wait()

        s = column_block(j, block)
        gate_sum[:, s] = jnp.dot(x_ref[...], gate_ref[:, s], preferred_element_type=F32)
        up_sum[:, s] = jnp.dot(x_ref[...], up_ref[:, s], preferred_element_type=F32)

    for copy in late:
        copy.wait()


def first_part(x0, x1, gate_v, up_v, gate, up, down, block, held, mine_block):
    rows, half = x0.shape
    ff = gate.shape[1]
    out = pl.pallas_call(
        functools.partial(first_kernel, block, held),
        out_shape=[pltpu.VMEM((2 * rows, ff), F32)] * 2
        + [pltpu.VMEM((half, ff), BF16)] * 2
        + [pltpu.VMEM((ff, mine_block), BF16), pltpu.VMEM((half, ff), BF16)],
        in_specs=[VMEM_SPEC] * 4 + [HBM_SPEC] * 3,
        out_specs=[VMEM_SPEC] * 6,
        scratch_shapes=[
            pltpu.VMEM((2 * rows, half), BF16),
            pltpu.SemaphoreType.DMA((3,)),
            pltpu.SemaphoreType.DMA((1,)),
        ],
        input_output_aliases={3: 5},
        compiler_params=pltpu.CompilerParams(vmem_limit_bytes=4 * 2**20),
        name="first",
    )(x0, x1, in_vmem(gate_v), in_vmem(up_v), in_hbm(gate), in_hbm(up), in_hbm(down))
    return out[:5]


def hidden_kernel(
    block, other_block, x0, x1, gate_sum, up_sum, gate_ref, up_ref, down_hbm,
    act_ref, keep_ref, send_ref, x_ref, other_ref, sems,
):
    rows, half = x0.shape
    other = down_copies(down_hbm, 1, other_block, 0, other_ref, sems)
    for j in range(half // other_block):
        other(j).start()
    x_ref[0:rows] = x0[...]
    x_ref[rows:] = x1[...]

    @pl.loop(0, gate_ref.shape[1] // block)
    def _(j):
        s = column_block(j, block)
        gate = gate_sum[:, s] + jnp.dot(x_ref[...], gate_ref[:, s], preferred_element_type=F32)
        up = up_sum[:, s] + jnp.dot(x_ref[...], up_ref[:, s], preferred_element_type=F32)
        act_ref[:, s] = (gate / (1.0 + jnp.exp(-gate)) * up).astype(BF16)

    @pl.loop(0, half // other_block)
    def _(j):
        other(j).wait()
        s = column_block(j, other_block)
        down_block(act_ref, other_ref[:, s], keep_ref, send_ref, s)


def hidden_part(x0, x1, gate_sum, up_sum, gate_v, up_v, down, block, other_block):
    rows, half = x0.shape
    ff = down.shape[0]
    return pl.pallas_call(
        functools.partial(hidden_kernel, block, other_block),
        out_shape=[
            pltpu.VMEM((2 * rows, ff), BF16),
            pltpu.VMEM((rows, half), F32),
            pltpu.VMEM((rows, half), BF16),
        ],
        in_specs=[VMEM_SPEC] * 6 + [HBM_SPEC],
        out_specs=[VMEM_SPEC] * 3,
        scratch_shapes=[
            pltpu.VMEM((2 * rows, half), BF16),
            pltpu.VMEM((ff, half), BF16),
            pltpu.SemaphoreType.DMA((half // other_block,)),
        ],
        compiler_params=pltpu.CompilerParams(vmem_limit_bytes=12 * 2**20),
        name="hidden",
    )(
        x0, x1, in_vmem(gate_sum), in_vmem(up_sum), in_vmem(gate_v), in_vmem(up_v), in_hbm(down)
    )


def down_kernel(act_ref, first_ref, down_hbm, keep_ref, send_ref, rest_ref, sems):
    block = first_ref.shape[1]
    blocks = keep_ref.shape[1] // block
    copy = down_copies(down_hbm, 0, block, 1, rest_ref, sems)
    for j in range(1, blocks):
        copy(j).start()
    down_block(act_ref, first_ref[...], keep_ref, send_ref, slice(0, block))

    @pl.loop(1, blocks)
    def _(j):
        copy(j).wait()
        rest = rest_ref[:, column_block(j - 1, block)]
        down_block(act_ref, rest, keep_ref, send_ref, column_block(j, block))


def down_part(act, down_v, down, half):
    rows, ff = act.shape[0] // 2, act.shape[1]
    block = down_v.shape[1]
    return pl.pallas_call(
        down_kernel,
        out_shape=[pltpu.VMEM((rows, half), F32), pltpu.VMEM((rows, half), BF16)],
        in_specs=[VMEM_SPEC, VMEM_SPEC, HBM_SPEC],
        out_specs=[VMEM_SPEC] * 2,
        scratch_shapes=[
            pltpu.VMEM((ff, half - block), BF16),
            pltpu.SemaphoreType.DMA((half // block,)),
        ],
        compiler_params=pltpu.CompilerParams(vmem_limit_bytes=8 * 2**20),
        name="down",
    )(in_vmem(act), in_vmem(down_v), in_hbm(down))


def combine_kernel(swaps, ids_ref, weights_ref, keep_ref, got_ref, hidden_ref, *refs):
    out_ref = refs[-1]
    me = lax.axis_index("expert")
    rows = out_ref.shape[0]
    ids, weights = ids_ref[...], weights_ref[...]

    def weighted(source, block):
        weight = jnp.sum(jnp.where(ids == source, weights, 0.0), axis=1, keepdims=True)
        return weight * block.astype(F32)

    own = keep_ref[0:rows] + got_ref[0:rows].astype(F32) + hidden_ref[...].astype(F32)
    total = weighted(me, own.astype(BF16))
    for by, ref in zip(swaps, refs[:-1]):
        total = total + weighted(me ^ by, ref[...])
    out_ref[...] = total.astype(BF16)


def combine(swaps, ids, weights, keep, got, from_hidden, arrived):
    return pl.pallas_call(
        functools.partial(combine_kernel, swaps),
        out_shape=jax.ShapeDtypeStruct(from_hidden.shape, BF16),
        in_specs=[VMEM_SPEC] * (5 + len(arrived)),
        out_specs=VMEM_SPEC,
        compiler_params=pltpu.CompilerParams(vmem_limit_bytes=4 * 2**20),
        name="combine",
    )(ids, weights, in_vmem(keep), in_vmem(got), in_vmem(from_hidden), *map(in_vmem, arrived))


def shards(tokens, expert_ids, gate_weights, w_gate, w_up, w_down):
    experts = lax.axis_size("expert")
    local_rows, half = tokens.shape
    gate, up, down = w_gate[0], w_up[0], w_down[0]
    block = gate.shape[1] // 4
    swaps = (*range(2, experts), 1)
    x00 = jnp.concatenate([tokens] + [swap(tokens, by) for by in swaps], axis=0)
    gate_v, up_v = load_part(gate, up, 5 * block // 2)
    x00, gate_v, up_v = lax.optimization_barrier((x00, gate_v, up_v))
    x10 = shift(x00, "request", 1)
    x01 = shift(x00, "hidden", 1)
    gate_sum, up_sum, gate_v, up_v, down_0 = first_part(
        x00, x10, gate_v, up_v, gate, up, down, 2 * block, 5 * block // 2, half // 3
    )
    x01, gate_sum = lax.optimization_barrier((x01, gate_sum))
    x11 = shift(x01, "request", 1)
    act, keep_other, send_other = hidden_part(
        x01, x11, gate_sum, up_sum, gate_v, up_v, down, 2 * block, half // 2
    )
    got_other = shift(send_other, "request", 1)
    sum_other = (keep_other + got_other.astype(F32)).astype(BF16)
    sum_other, act = lax.optimization_barrier((sum_other, act))
    from_hidden = shift(sum_other[local_rows:], "hidden", 1)
    keep_mine, send_mine = down_part(act, down_0, down, half)
    own_other, keep_mine = lax.optimization_barrier((sum_other[:local_rows], keep_mine))
    own_from_hidden = shift(own_other, "hidden", 1)
    got_mine = shift(send_mine, "request", 1)
    away = lax.optimization_barrier(keep_mine[local_rows:] + from_hidden.astype(F32))
    away = (away + got_mine[local_rows:].astype(F32)).astype(BF16)
    away = away.reshape(experts - 1, local_rows, half)
    back = (experts - 1, *range(1, experts - 1))
    arrived = [swap(away[swaps.index(by)], by) for by in back]
    return combine(
        back, expert_ids, gate_weights, keep_mine, got_mine, own_from_hidden, arrived
    )


def shards_any(tokens, expert_ids, gate_weights, w_gate, w_up, w_down):
    experts, requests, slices = (lax.axis_size(a) for a in ("expert", "request", "hidden"))
    local_rows, width = tokens.shape
    rows = lax.all_gather(tokens, "hidden", axis=1, tiled=True)
    rows = lax.all_gather(rows, ("expert", "request"), axis=0, tiled=True)
    gate = jnp.dot(rows, w_gate[0], preferred_element_type=F32)
    up = jnp.dot(rows, w_up[0], preferred_element_type=F32)
    act = (jax.nn.silu(gate) * up).astype(BF16)
    out = jnp.dot(act, w_down[0], preferred_element_type=F32)
    out = out.reshape(experts, requests, local_rows, slices, width)
    out = out.transpose(3, 1, 0, 2, 4).reshape(slices * requests, experts * local_rows, width)
    out = lax.psum_scatter(out, ("hidden", "request"), scatter_dimension=0, tiled=True)
    out = out.reshape(experts, local_rows, width).astype(BF16)
    out = lax.all_to_all(out, "expert", split_axis=0, concat_axis=0, tiled=True)
    chosen = expert_ids[:, :, None] == jnp.arange(experts, dtype=jnp.int32)
    weights = jnp.sum(jnp.where(chosen, gate_weights[:, :, None], 0.0), axis=1)
    combined = jnp.sum(weights.T[:, :, None] * out.astype(F32), axis=0)
    return combined.astype(BF16)


def solution(mesh):
    experts = mesh.shape["expert"]
    halves = mesh.shape["hidden"] == 2 and mesh.shape["request"] == 2
    halves = halves and experts & (experts - 1) == 0
    return jax.shard_map(
        shards if halves else shards_any,
        mesh=mesh,
        in_specs=(
            P(("replica", "expert", "request"), "hidden"),
            P(("replica", "expert", "request"), None),
            P(("replica", "expert", "request"), None),
            P("expert", None, ("hidden", "request")),
            P("expert", None, ("hidden", "request")),
            P("expert", ("hidden", "request"), None),
        ),
        out_specs=P(("replica", "expert", "request"), "hidden"),
        check_vma=False,
    )
```
